32 devices in a mesh: grp: 4 (over y, core), blk: 8 (over z, x).
Axes of the slice: x: 2, y: 2, z: 4, core: 2. Of those that a mesh axis runs over, the one named last changes fastest.
Arguments:
- hidden_in: bfloat16 [8, 512, 1024], P('blk', 'grp'), may hold values from -6 to 6
- attn_gain: float32 [1024], replicated, may hold values from 0.1 to 1.9
- qkv_weight: bfloat16 [1024, 3, 16, 64], P(None, None, 'grp'), may hold values from -0.09375 to 0.09375
- rel_bias: float32 [32, 16], P(None, 'grp'), may hold values from -4 to 4
- prefix_cache: bfloat16 [8, 256, 2, 16, 64], P('blk', None, None, 'grp'), may hold values from -34 to 34
- prefix_owner: int32 [8], replicated, may hold values from 0 to 7, each once
- req_prefix: int32 [8, 2], replicated, may hold values from 0 to 7
- req_pages: int32 [8, 2], replicated, may hold values from 1 to 12, 16 in all within a row
- page_table: int32 [8, 16], replicated, may hold values from 0 to 15, each once within a row
- proj_weight: bfloat16 [1024, 1024], replicated, may hold values from -0.1875 to 0.1875
- mlp_gain: float32 [1024], replicated, may hold values from 0.1 to 1.9
- in_weight: bfloat16 [1024, 4096], P(None, 'grp'), may hold values from -0.1875 to 0.1875
- out_weight: bfloat16 [4096, 1024], P('grp'), may hold values from -0.09375 to 0.09375
Outputs:
- hidden_out: bfloat16 [8, 512, 1024], P('blk', 'grp')
- suffix_cache: bfloat16 [8, 512, 2, 16, 64], P('blk', None, None, 'grp')
The draws below stay inside these ranges and needn't reach their ends.
Inputs may be any that keep to these rules, and one draw needn't show every extreme that they name: Prefix p's keys and values are row prefix_owner[p] of prefix_cache; every owner column holds one prefix. `req_pages`: each row sums to 16 and no entry exceeds 12. `page_table`: each row is a permutation of the logical pages of a column.
All inputs are finite; a program needn't handle non-finite values.
Results may differ from the reference program's by a relative error of at most 0.012.
Values may be sent and summed in bfloat16 or wider, within the bound.
A program may use at most 128 MiB of HBM per device.

```python
import math
import jax
import jax.numpy as jnp
import numpy as np
from jax import lax

D = 1024
HEADS = 16
DK = 64
FF = 4096
BUCKETS = 32
REQ_COL = 2
PAGE = 32
PLEN = 256
PAGES_COL = 16
COL_TOK = 512
MOST = 12
PREFIXES = 8
TOKENS = 4096
N_GRP = 4
N_BLK = 8


def draw_prefix_cache(key, part):
    key_base = jax.random.fold_in(key, 0)
    shape = (PREFIXES, PLEN, 2, HEADS, DK)
    base = jnp.clip(jax.random.normal(key_base, shape, jnp.float32) * 0.5, -3.0, 3.0)
    return base.astype(jnp.bfloat16)


def place_ends(array, own_key, smallest, largest):
    longest = array.shape.index(max(array.shape))
    spots = []
    for shift in (0, 1):
        where = [jax.random.randint(jax.random.fold_in(own_key, axis), (), 0, length) for axis, length in enumerate(array.shape)]
        where[longest] = (where[longest] + shift) % array.shape[longest]
        spots.append(tuple(where))
    return array.at[spots[0]].set(smallest).at[spots[1]].set(largest)


def steps_of(own_key, shape, cuts, low, high):
    loudness, own = 1.0, jax.random.fold_in(own_key, 6)
    for position, parts in cuts:
        heights = jnp.exp(jax.random.uniform(jax.random.fold_in(own, position), (parts,), jnp.float32, low / len(cuts), high / len(cuts)))
        loudness = loudness * jnp.repeat(heights, shape[position] // parts).reshape([-1 if axis == position else 1 for axis in range(len(shape))])
    return loudness


def profile(number_of, total, most, lean):
    loads = [(1 << 20) // math.isqrt(standing ** lean) + 1 for standing in range(2, number_of + 1)]
    spare, given = total - most - (number_of - 1), [1] * (number_of - 1)
    while spare > 0:
        movable = [i for i in range(number_of - 1) if given[i] < most]
        mass, remaining = sum([loads[i] for i in movable]), spare
        for i in movable:
            extra = min(most - given[i], max(1, remaining * loads[i] // mass), spare)
            given[i] = given[i] + extra
            spare = spare - extra
    return np.array([most] + given)


def uneven(own_key, number_of, total, most, lean):
    if number_of == 2:
        one = jax.random.randint(own_key, (), max(1, total - most), min(most, total - 1) + 1)
        return jnp.stack([one, total - one])
    lengths = jnp.asarray(profile(number_of, total, most, lean), jnp.int32)
    pairs = (number_of - 1) // 2
    donor, receiver = lengths[1:1 + 2 * pairs:2], lengths[2:2 + 2 * pairs:2]
    room = jnp.minimum(donor - 1, most - receiver)
    passed = jax.random.randint(jax.random.fold_in(own_key, 1), (pairs,), 0, 1 << 20) % (room + 1)
    lengths = lengths.at[1:1 + 2 * pairs:2].set(donor - passed).at[2:2 + 2 * pairs:2].set(receiver + passed)
    return lengths[jax.random.permutation(jax.random.fold_in(own_key, 2), number_of)]


def scatter_about(stream_key, extent, spread, bound, cuts=(), kind=jnp.bfloat16):
    level = steps_of(stream_key, extent, cuts, -0.22, 0.18) if cuts else 1.0
    result = jax.random.normal(stream_key, extent, jnp.float32) * spread * level
    return jnp.minimum(jnp.maximum(result, -bound), bound).astype(kind)


def setup_inputs(seed: int = 0) -> dict:
    streams_of = jax.random.split(jax.random.key(seed), 14)
    hidden_in = scatter_about(streams_of[0], (N_BLK, COL_TOK, D), 1.0, 6.0, ((0, 8), (1, 4)))
    attn_gain = jnp.clip(1.0 + 0.18 * jax.random.normal(streams_of[1], (D,), jnp.float32), 0.1, 1.9)
    qkv_weight = scatter_about(streams_of[2], (D, 3, HEADS, DK), (4 * D) ** -0.5, 0.09375, ((2, 4),))
    rel_bias = scatter_about(streams_of[3], (BUCKETS, HEADS), 1.0, 4.0, ((1, 4),), jnp.float32)
    prefix_cache = draw_prefix_cache(jax.random.fold_in(streams_of[13], 71), 0)
    prefix_owner = jax.random.permutation(streams_of[5], N_BLK).astype(jnp.int32)
    req_prefix = place_ends(jax.random.randint(streams_of[6], (N_BLK, REQ_COL), 0, PREFIXES), jax.random.fold_in(streams_of[6], 1), 0, PREFIXES - 1).astype(jnp.int32)
    req_pages = jax.vmap(lambda own: uneven(own, REQ_COL, PAGES_COL, MOST, 2))(jax.random.split(streams_of[7], N_BLK)).reshape((N_BLK, REQ_COL)).astype(jnp.int32)
    page_table = jax.vmap(lambda own: jax.random.permutation(own, PAGES_COL))(jax.random.split(streams_of[8], N_BLK)).reshape((N_BLK, PAGES_COL)).astype(jnp.int32)
    proj_weight = scatter_about(streams_of[9], (HEADS * DK, D), (HEADS * DK) ** -0.5, 0.1875)
    mlp_gain = jnp.clip(1.0 + 0.18 * jax.random.normal(streams_of[10], (D,), jnp.float32), 0.1, 1.9)
    in_weight = scatter_about(streams_of[11], (D, FF), D ** -0.5, 0.1875, ((1, 4),))
    out_weight = scatter_about(streams_of[12], (FF, D), FF ** -0.5, 0.09375, ((0, 4),))
    return dict(hidden_in=hidden_in, attn_gain=attn_gain, qkv_weight=qkv_weight, rel_bias=rel_bias, prefix_cache=prefix_cache, prefix_owner=prefix_owner, req_prefix=req_prefix, req_pages=req_pages, page_table=page_table, proj_weight=proj_weight, mlp_gain=mlp_gain, in_weight=in_weight, out_weight=out_weight)


EPSILON = 1e-06
THRESHOLDS = (12, 16, 23, 32, 46, 64, 91)

def rms_scale(values, gain):
    mean_sq = lax.optimization_barrier(jnp.mean(values * values, axis=-1, keepdims=True))
    return values * lax.rsqrt(mean_sq + EPSILON) * gain.astype(jnp.float32)

def bucket_of(relative):
    magnitude = jnp.abs(relative)
    steps_up = jnp.zeros(relative.shape, jnp.int32)
    for limit in THRESHOLDS:
        steps_up = steps_up + (magnitude >= limit).astype(jnp.int32)
    bucket = jnp.where(magnitude < 8, magnitude, jnp.minimum(8 + steps_up, 15))
    return (bucket + 16 * (relative > 0).astype(jnp.int32)).astype(jnp.int32)

def token_meta(pages_row, lengths_row, page_size, prefix_len):
    inclusive = jnp.cumsum(lengths_row, dtype=jnp.int32)
    exclusive = inclusive - lengths_row
    request = lax.optimization_barrier(jnp.sum((pages_row[:, None] >= inclusive[None, :]).astype(jnp.int32), axis=1, dtype=jnp.int32))
    slot_ids = jnp.arange(lengths_row.shape[0], dtype=jnp.int32)
    start = lax.optimization_barrier(jnp.sum(jnp.where(request[:, None] == slot_ids[None, :], exclusive[None, :], 0), axis=1, dtype=jnp.int32))
    offsets = (pages_row - start) * page_size + prefix_len
    within = jnp.arange(page_size, dtype=jnp.int32)
    positions = (offsets[:, None] + within[None, :]).reshape(-1).astype(jnp.int32)
    requests = jnp.broadcast_to(request[:, None], (request.shape[0], page_size)).reshape(-1).astype(jnp.int32)
    return (requests, positions)

def attend_block(queries, key_rows, value_rows, query_req, query_pos, key_req, key_pos, rel_bias):
    scores = jnp.einsum('qhd,khd->hqk', queries.astype(jnp.float32), key_rows.astype(jnp.float32))
    bucket = bucket_of(key_pos[None, :] - query_pos[:, None])
    bias_add = jnp.transpose(jnp.take(rel_bias, bucket, axis=0), (2, 0, 1))
    allowed = (key_req[None, :] == query_req[:, None])[None]
    scores = jnp.where(allowed, scores + bias_add, -1e+30)
    row_max = lax.optimization_barrier(jnp.max(scores, axis=-1, keepdims=True))
    weights = jnp.exp(scores - row_max)
    weights = (weights / lax.optimization_barrier(jnp.sum(weights, axis=-1, keepdims=True))).astype(jnp.bfloat16)
    return jnp.einsum('hqk,khd->qhd', weights.astype(jnp.float32), value_rows.astype(jnp.float32)).astype(jnp.bfloat16)

def reference(hidden_in, attn_gain, qkv_weight, rel_bias, prefix_cache, prefix_owner, req_prefix, req_pages, page_table, proj_weight, mlp_gain, in_weight, out_weight):
    residual = hidden_in.astype(jnp.float32).reshape(TOKENS, D)
    normed = rms_scale(residual, attn_gain).astype(jnp.bfloat16)
    projected = jnp.dot(normed, qkv_weight.reshape(D, 3 * HEADS * DK), preferred_element_type=jnp.float32)
    projected = projected.astype(jnp.bfloat16).reshape(N_BLK, COL_TOK, 3, HEADS, DK)
    suffix_cache = projected[:, :, 1:3]
    owner_cols = jnp.take(prefix_owner, req_prefix, axis=0).astype(jnp.int32)
    block_rows = min(512, COL_TOK)

    def per_column(operands):
        cols_row, pages_row, lengths_row, column_qkv = operands
        prefix_rows = jnp.take(prefix_cache, cols_row, axis=0).reshape(REQ_COL * PLEN, 2, HEADS, DK)
        key_rows = jnp.concatenate([prefix_rows[:, 0], column_qkv[:, 1]], axis=0)
        value_rows = jnp.concatenate([prefix_rows[:, 1], column_qkv[:, 2]], axis=0)
        query_req, query_pos = token_meta(pages_row, lengths_row, PAGE, PLEN)
        slot_ids = jnp.arange(REQ_COL, dtype=jnp.int32)
        key_req = jnp.concatenate([jnp.repeat(slot_ids, PLEN), query_req])
        key_pos = jnp.concatenate([jnp.tile(jnp.arange(PLEN, dtype=jnp.int32), REQ_COL), query_pos])
        outputs = []
        for first in range(0, COL_TOK, block_rows):
            outputs.append(attend_block(column_qkv[first:first + block_rows, 0], key_rows, value_rows, query_req[first:first + block_rows], query_pos[first:first + block_rows], key_req, key_pos, rel_bias))
        return jnp.concatenate(outputs, axis=0).reshape(COL_TOK, HEADS * DK)
    attended = lax.map(per_column, (owner_cols, page_table, req_pages, projected))
    mixed = residual + jnp.dot(attended.reshape(TOKENS, HEADS * DK), proj_weight, preferred_element_type=jnp.float32)
    normed_mlp = rms_scale(mixed, mlp_gain).astype(jnp.bfloat16)
    activated = jax.nn.relu(jnp.dot(normed_mlp, in_weight, preferred_element_type=jnp.float32)).astype(jnp.bfloat16)
    units = FF // N_GRP

    def add_share(share, total):
        first = (share * units).astype(jnp.int32)
        part = jnp.dot(lax.dynamic_slice_in_dim(activated, first, units, 1), lax.dynamic_slice_in_dim(out_weight, first, units, 0), preferred_element_type=jnp.float32)
        rounded = lax.optimization_barrier(part.astype(jnp.bfloat16))
        return total + rounded.astype(jnp.float32)
    summed = lax.fori_loop(0, N_GRP, add_share, jnp.zeros((TOKENS, D), jnp.float32))
    hidden_out = (mixed + summed).astype(jnp.bfloat16).reshape(N_BLK, COL_TOK, D)
    return (hidden_out, suffix_cache)
```

```python
import jax
import jax.numpy as jnp
from jax import lax
from jax.experimental import pallas as pl
from jax.experimental.pallas import tpu as pltpu
from jax.sharding import PartitionSpec as P

PAGE = 32


EPSILON = 1e-06
THRESHOLDS = (12, 16, 23, 32, 46, 64, 91)


def rms_scale(values, gain):
    mean_sq = jnp.mean(values * values, axis=-1, keepdims=True)
    return values * lax.rsqrt(mean_sq + EPSILON) * gain


def bucket_of(relative):
    magnitude = jnp.abs(relative)
    steps_up = jnp.zeros(relative.shape, jnp.int32)
    for limit in THRESHOLDS:
        steps_up = steps_up + (magnitude >= limit).astype(jnp.int32)
    bucket = jnp.where(magnitude < 8, magnitude, jnp.minimum(8 + steps_up, 15))
    return bucket + 16 * (relative > 0).astype(jnp.int32)


def token_meta(pages_row, lengths_row, page_size, prefix_len):
    order = jnp.arange(lengths_row.shape[0], dtype=jnp.int32)
    inclusive = jnp.sum(
        jnp.where(order[None, :] <= order[:, None], lengths_row[None, :], 0), axis=1, dtype=jnp.int32
    )
    exclusive = inclusive - lengths_row
    request = jnp.sum(
        (pages_row[:, None] >= inclusive[None, :]).astype(jnp.int32), axis=1, dtype=jnp.int32
    )
    slot_ids = jnp.arange(lengths_row.shape[0], dtype=jnp.int32)
    start = jnp.sum(
        jnp.where(request[:, None] == slot_ids[None, :], exclusive[None, :], 0),
        axis=1,
        dtype=jnp.int32,
    )
    offsets = (pages_row - start) * page_size + prefix_len
    within = jnp.arange(page_size, dtype=jnp.int32)
    positions = (offsets[:, None] + within[None, :]).reshape(-1)
    requests = jnp.broadcast_to(request[:, None], (request.shape[0], page_size)).reshape(-1)
    return (requests, positions)


def attend_block(queries, key_rows, value_rows, query_req, query_pos, key_req, key_pos, rel_bias):
    scores = jnp.einsum("qhd,khd->hqk", queries, key_rows, preferred_element_type=jnp.float32)
    bucket = bucket_of(key_pos[None, :] - query_pos[:, None])
    bias_add = jnp.zeros(scores.shape, jnp.float32)
    for bucket_id in range(rel_bias.shape[0]):
        bias_add = jnp.where(
            (bucket == bucket_id)[None], rel_bias[bucket_id][:, None, None], bias_add
        )
    allowed = (key_req[None, :] == query_req[:, None])[None]
    scores = jnp.where(allowed, scores + bias_add, -1e30)
    row_max = jnp.max(scores, axis=-1, keepdims=True)
    weights = jnp.exp(scores - row_max)
    weights = (weights / jnp.sum(weights, axis=-1, keepdims=True)).astype(jnp.bfloat16)
    return jnp.einsum(
        "hqk,khd->qhd", weights, value_rows, preferred_element_type=jnp.float32
    ).astype(jnp.bfloat16)


def shards(
    hidden_in,
    attn_gain,
    qkv_weight,
    rel_bias,
    prefix_cache,
    prefix_owner,
    req_prefix,
    req_pages,
    page_table,
    proj_weight,
    mlp_gain,
    in_weight,
    out_weight,
):
    width = hidden_in.shape[2]
    heads_dev = qkv_weight.shape[2]
    head_dim = qkv_weight.shape[3]
    inner = heads_dev * head_dim
    residual = hidden_in[0].astype(jnp.float32)
    normed = rms_scale(residual, attn_gain).astype(jnp.bfloat16)
    qkv_flat = qkv_weight.reshape(width, 3 * inner)
    projected = jnp.dot(
        lax.all_gather(normed, "grp", axis=0, tiled=True),
        qkv_flat,
        preferred_element_type=jnp.float32,
    ).astype(jnp.bfloat16)
    column_tok = projected.shape[0]
    projected = projected.reshape(column_tok, 3, heads_dev, head_dim)
    suffix_cache = projected[:, 1:3][None]
    column = lax.axis_index("blk")
    requests_col = req_prefix.shape[1]
    prefix_ids = jnp.arange(prefix_owner.shape[0], dtype=jnp.int32)
    owner_cols = jnp.sum(
        jnp.where(
            req_prefix[:, :, None] == prefix_ids[None, None, :], prefix_owner[None, None, :], 0
        ),
        axis=2,
        dtype=jnp.int32,
    )
    my_cols = lax.dynamic_index_in_dim(owner_cols, column, 0, keepdims=False)
    prefix_len = prefix_cache.shape[1]
    slot_width = 2 * inner
    local_slot = prefix_cache.reshape(prefix_len, slot_width)
    gathered = lax.all_gather(local_slot[None], "blk", axis=0, tiled=True)
    prefix_rows = jnp.stack(
        [
            lax.dynamic_index_in_dim(gathered, my_cols[k], 0, keepdims=False)
            for k in range(requests_col)
        ]
    )
    prefix_rows = prefix_rows.reshape(requests_col * prefix_len, 2, heads_dev, head_dim)
    key_rows = jnp.concatenate([prefix_rows[:, 0], projected[:, 1]], axis=0)
    value_rows = jnp.concatenate([prefix_rows[:, 1], projected[:, 2]], axis=0)
    pages_row = lax.dynamic_index_in_dim(page_table, column, 0, keepdims=False)
    lengths_row = lax.dynamic_index_in_dim(req_pages, column, 0, keepdims=False)
    query_req, query_pos = token_meta(pages_row, lengths_row, PAGE, prefix_len)
    slot_ids = jnp.arange(requests_col, dtype=jnp.int32)
    key_req = jnp.concatenate([jnp.repeat(slot_ids, prefix_len), query_req])
    key_pos = jnp.concatenate(
        [jnp.tile(jnp.arange(prefix_len, dtype=jnp.int32), requests_col), query_pos]
    )
    block_rows = min(512, column_tok)
    block_count = column_tok // block_rows

    def one_block(operands):
        block_q, block_req, block_pos = operands
        return attend_block(
            block_q, key_rows, value_rows, block_req, block_pos, key_req, key_pos, rel_bias
        )

    attended = lax.map(
        one_block,
        (
            projected[:, 0].reshape(block_count, block_rows, heads_dev, head_dim),
            query_req.reshape(block_count, block_rows),
            query_pos.reshape(block_count, block_rows),
        ),
    )
    attended = attended.reshape(1, column_tok, inner)
    token_heads = lax.all_to_all(attended, "grp", split_axis=1, concat_axis=2, tiled=True)[0]
    mixed = residual + jnp.dot(token_heads, proj_weight, preferred_element_type=jnp.float32)
    normed_mlp = rms_scale(mixed, mlp_gain).astype(jnp.bfloat16)
    activated = jax.nn.relu(
        jnp.dot(
            lax.all_gather(normed_mlp, "grp", axis=0, tiled=True),
            in_weight,
            preferred_element_type=jnp.float32,
        )
    ).astype(jnp.bfloat16)
    summed = lax.psum_scatter(
        jnp.dot(activated, out_weight, preferred_element_type=jnp.float32).astype(jnp.bfloat16),
        "grp",
        scatter_dimension=0,
        tiled=True,
    ).astype(jnp.float32)
    hidden_out = (mixed + summed).astype(jnp.bfloat16)[None]
    return (hidden_out, suffix_cache)


MESH = pl.DeviceIdType.MESH
TILE = 128


def remote(src, dst, send, recv, where):
    return pltpu.make_async_remote_copy(
        src_ref=src, dst_ref=dst, send_sem=send, recv_sem=recv, device_id=where, device_id_type=MESH
    )


def grp_places():
    me = lax.axis_index("grp")
    y, core = me // 2, me % 2
    return me, y * 2 + 1 - core, (1 - y) * 2 + core, (1 - y) * 2 + 1 - core


def rms_rows(values, gain):
    mean_sq = jnp.mean(values * values, axis=-1, keepdims=True)
    return (values * lax.rsqrt(mean_sq + EPSILON) * gain).astype(jnp.bfloat16)


def qkv_kernel(
    hidden, gain, weight, prefix, owner, req_prefix,
    qkv, picked,
    states, slots, g_send, g_recv, r_send, r_recv, l_send, l_recv, x_send, x_recv, own_sem,
):
    me, mate, across, diag = grp_places()
    blk = lax.axis_index("blk")
    z, x = blk // 2, blk % 2
    other = z * 2 + 1 - x
    mine = pltpu.make_async_copy(prefix, slots.at[blk], own_sem)
    mine.start()
    barrier = pltpu.get_barrier_semaphore()
    for place in ({"grp": mate}, {"grp": across}, {"blk": other},
                  {"blk": (z + 1) % 4 * 2 + x}, {"blk": (z + 3) % 4 * 2 + x}):
        pl.semaphore_signal(barrier, inc=1, device_id=place, device_id_type=MESH)
    pl.semaphore_wait(barrier, 5)
    mine.wait()

    def up(slot, s):
        ref = slots.at[slot * 2 + x]
        return remote(ref, ref, r_send.at[s], r_recv.at[s], {"blk": (z + 1) % 4 * 2 + x})

    def down(slot, s):
        ref = slots.at[slot * 2 + x]
        return remote(ref, ref, l_send.at[s], l_recv.at[s], {"blk": (z + 3) % 4 * 2 + x})

    def over(slot, side):
        ref = slots.at[slot * 2 + side]
        return remote(ref, ref, x_send.at[slot], x_recv.at[slot], {"blk": other})

    def hop(s):
        @pl.when((z < 3) & (z >= s))
        def _():
            up(z - s, s).start()

        @pl.when((z > 0) & (z + s <= 3))
        def _():
            down(z + s, s).start()

    def land(s):
        @pl.when(z >= s + 1)
        def _():
            up(z - 1 - s, s).wait_recv()

        @pl.when(z + s + 1 <= 3)
        def _():
            down(z + 1 + s, s).wait_recv()

        if s < 2:
            hop(s + 1)

        @pl.when(z >= s + 1)
        def _():
            over(z - 1 - s, x).start()

        @pl.when(z + s + 1 <= 3)
        def _():
            over(z + 1 + s, x).start()

    hop(0)
    over(z, x).start()
    states[me] = rms_rows(hidden[...].astype(jnp.float32), gain[...])
    to_mate = remote(states.at[me], states.at[me], g_send.at[0], g_recv.at[0], {"grp": mate})
    to_across = remote(states.at[me], states.at[me], g_send.at[1], g_recv.at[1], {"grp": across})
    to_across.start()
    to_mate.start()

    def project(place):
        rows = pl.ds(pl.multiple_of(place * TILE, TILE), TILE)
        qkv[rows, :] = jnp.dot(
            states[place], weight[...], preferred_element_type=jnp.float32
        ).astype(jnp.bfloat16)

    project(me)
    remote(states.at[mate], states.at[mate], g_send.at[0], g_recv.at[0], {"grp": mate}).wait_recv()
    project(mate)
    remote(states.at[across], states.at[across], g_send.at[1], g_recv.at[1], {"grp": across}).wait_recv()
    onward = remote(states.at[across], states.at[across], g_send.at[2], g_recv.at[2], {"grp": mate})
    onward.start()
    land(0)
    project(across)
    remote(states.at[diag], states.at[diag], g_send.at[2], g_recv.at[2], {"grp": mate}).wait_recv()
    project(diag)
    land(1)
    land(2)
    for slot in range(4):
        over(slot, 1 - x).wait_recv()
    for k in range(2):
        picked[k] = slots[owner[req_prefix[blk, k]]]
    to_mate.wait_send()
    to_across.wait_send()
    onward.wait_send()
    for s in range(3):
        @pl.when((z < 3) & (z >= s))
        def _():
            up(z - s, s).wait_send()

        @pl.when((z > 0) & (z + s <= 3))
        def _():
            down(z + s, s).wait_send()
    for slot in range(4):
        over(slot, x).wait_send()


def attend_kernel(qkv, picked, pages, lengths, rel_bias, out, ordered, result, tiles, shifted):
    blk = lax.axis_index("blk")
    tokens, inner = out.shape
    page_count = tokens // PAGE
    heads = rel_bias.shape[1]
    dim = inner // heads
    split = lengths[blk, 0] * PAGE
    row = lax.broadcasted_iota(jnp.int32, (TILE, TILE), 0)
    col = lax.broadcasted_iota(jnp.int32, (TILE, TILE), 1)

    @pl.loop(1, 4)
    def _(d):
        bucket = bucket_of((d - 2) * TILE + col - row)
        sums = [jnp.zeros((TILE, TILE), jnp.float32)] * heads
        for b in range(rel_bias.shape[0]):
            here = bucket == b
            sums = [jnp.where(here, rel_bias[b, h], sums[h]) for h in range(heads)]
        for h in range(heads):
            tiles[h, d] = sums[h]

    for h in range(heads):
        tiles[h, 0] = jnp.full((TILE, TILE), rel_bias[15, h], jnp.float32)
        tiles[h, 4] = jnp.full((TILE, TILE), rel_bias[31, h], jnp.float32)
        shifted[h] = jnp.full((2 * tokens, TILE), rel_bias[15, h], jnp.float32)
        shifted[h, tokens:tokens + TILE] = tiles[h, 1]

    @pl.loop(0, page_count)
    def _(logical):
        physical = jnp.int32(0)
        for j in range(page_count):
            physical = physical + jnp.where(pages[blk, j] == logical, j, 0)
        ordered[pl.ds(pl.multiple_of(logical * PAGE, PAGE), PAGE), :] = qkv[
            pl.ds(pl.multiple_of(physical * PAGE, PAGE), PAGE), :
        ]

    blocks = tokens // TILE
    key_late = lax.broadcasted_iota(jnp.int32, (TILE, tokens), 1) >= split

    @pl.loop(0, blocks)
    def _(i):
        rows = pl.ds(pl.multiple_of(i * TILE, TILE), TILE)
        number = i * TILE + lax.broadcasted_iota(jnp.int32, (TILE, tokens), 0)
        allowed = (number >= split) == key_late
        late = i * TILE + lax.broadcasted_iota(jnp.int32, (TILE, 2 * TILE), 0) >= split
        shift = pl.multiple_of(tokens + i * TILE - split, PAGE)
        contract = (((1,), (1,)), ((), ()))
        for h in range(heads):
            at = slice(h * dim, (h + 1) * dim)
            key_at = slice(inner + h * dim, inner + (h + 1) * dim)
            value_at = slice(2 * inner + h * dim, 2 * inner + (h + 1) * dim)
            q = ordered[rows, at]

            def against(keys):
                return lax.dot_general(q, keys, contract, preferred_element_type=jnp.float32)

            own = against(ordered[:, key_at])
            bias = jnp.concatenate(
                [tiles[h, jnp.clip(j - i, -2, 2) + 2] for j in range(blocks)], axis=1
            )
            own = jnp.where(allowed, own + bias, -1e30)
            far = jnp.full((TILE, TILE), rel_bias[15, h], jnp.float32)
            early = jnp.concatenate([far, tiles[h, jnp.maximum(1 - i, 0)]], axis=1)
            later = jnp.concatenate([far, shifted[h, pl.ds(shift, TILE), :]], axis=1)
            before = jnp.where(
                late, against(picked[1, :, at]) + later, against(picked[0, :, at]) + early
            )
            top = jnp.maximum(
                jnp.max(own, axis=1, keepdims=True), jnp.max(before, axis=1, keepdims=True)
            )
            own = jnp.exp(own - top)
            before = jnp.exp(before - top)
            total = jnp.sum(own, axis=1, keepdims=True) + jnp.sum(before, axis=1, keepdims=True)
            summed = jnp.dot(
                own.astype(jnp.bfloat16), ordered[:, value_at], preferred_element_type=jnp.float32
            )
            for k in range(2):
                part = jnp.where(late == (k == 1), before, 0.0).astype(jnp.bfloat16)
                summed = summed + jnp.dot(
                    part, picked[k, :, key_at], preferred_element_type=jnp.float32
                )
            result[rows, at] = (summed / total).astype(jnp.bfloat16)

    @pl.loop(0, page_count)
    def _(j):
        out[pl.ds(pl.multiple_of(j * PAGE, PAGE), PAGE), :] = result[
            pl.ds(pl.multiple_of(pages[blk, j] * PAGE, PAGE), PAGE), :
        ]


def mlp_kernel(
    hidden, attended, proj_hbm, gain, in_hbm, out_hbm,
    final,
    proj, in_w, out_w, heads_in, states, mixed, total, leaving, arriving,
    w_sem, a_send, a_recv, g_send, g_recv, s_send, s_recv,
):
    me, mate, across, diag = grp_places()
    loads = [
        pltpu.make_async_copy(a, b, w_sem.at[k])
        for k, (a, b) in enumerate(((proj_hbm, proj), (in_hbm, in_w), (out_hbm, out_w)))
    ]
    for load in loads:
        load.start()
    barrier = pltpu.get_barrier_semaphore()
    for place in (mate, across, diag):
        pl.semaphore_signal(barrier, inc=1, device_id={"grp": place}, device_id_type=MESH)
    pl.semaphore_wait(barrier, 3)

    def rows_of(place):
        return pl.ds(pl.multiple_of(place * TILE, TILE), TILE)

    def share_out(k, place):
        return remote(
            attended.at[rows_of(place), :], heads_in.at[me], a_send.at[k], a_recv.at[k], {"grp": place}
        )

    def share_in(k, place):
        return remote(
            attended.at[rows_of(place), :], heads_in.at[place], a_send.at[k], a_recv.at[k], {"grp": place}
        )

    peers = ((1, across), (2, diag), (0, mate))
    for k, place in peers:
        share_out(k, place).start()
    depth = attended.shape[1]

    def mix(block, place):
        return jnp.dot(
            block,
            proj[pl.ds(pl.multiple_of(place * depth, depth), depth), :],
            preferred_element_type=jnp.float32,
        )

    loads[0].wait()
    mixed[...] = hidden[...].astype(jnp.float32) + mix(attended[rows_of(me), :], me)
    for k, place in ((0, mate), (1, across), (2, diag)):
        share_in(k, place).wait_recv()
        mixed[...] += mix(heads_in[place], place)
    states[me] = rms_rows(mixed[...], gain[...])
    to_mate = remote(states.at[me], states.at[me], g_send.at[0], g_recv.at[0], {"grp": mate})
    to_across = remote(states.at[me], states.at[me], g_send.at[1], g_recv.at[1], {"grp": across})
    to_across.start()
    to_mate.start()
    loads[1].wait()
    loads[2].wait()

    def share(place):
        hidden_units = jnp.dot(states[place], in_w[...], preferred_element_type=jnp.float32)
        activated = jnp.maximum(hidden_units, 0.0).astype(jnp.bfloat16)
        return jnp.dot(activated, out_w[...], preferred_element_type=jnp.float32)

    def give(k, place):
        return remote(leaving.at[k], arriving.at[k], s_send.at[k], s_recv.at[k], {"grp": place})

    total[...] = share(me)
    remote(states.at[mate], states.at[mate], g_send.at[0], g_recv.at[0], {"grp": mate}).wait_recv()
    leaving[0] = share(mate).astype(jnp.bfloat16)
    give(0, mate).start()
    total[...] += mixed[...]
    remote(states.at[across], states.at[across], g_send.at[1], g_recv.at[1], {"grp": across}).wait_recv()
    onward = remote(states.at[across], states.at[across], g_send.at[2], g_recv.at[2], {"grp": mate})
    onward.start()
    mixed[...] = share(across)
    remote(states.at[diag], states.at[diag], g_send.at[2], g_recv.at[2], {"grp": mate}).wait_recv()
    leaving[1] = share(diag).astype(jnp.bfloat16)
    give(1, mate).start()
    give(1, mate).wait_recv()
    leaving[2] = (mixed[...] + arriving[1].astype(jnp.float32)).astype(jnp.bfloat16)
    give(2, across).start()
    give(0, mate).wait_recv()
    total[...] += arriving[0].astype(jnp.float32)
    give(2, across).wait_recv()
    final[...] = (total[...] + arriving[2].astype(jnp.float32)).astype(jnp.bfloat16)
    for k, place in peers:
        share_out(k, place).wait_send()
    to_mate.wait_send()
    to_across.wait_send()
    onward.wait_send()
    give(0, mate).wait_send()
    give(1, mate).wait_send()
    give(2, across).wait_send()


VMEM = pl.BlockSpec(memory_space=pltpu.VMEM)
SMEM = pl.BlockSpec(memory_space=pltpu.SMEM)
HBM = pl.BlockSpec(memory_space=pl.ANY)
LIMIT = 48 * 2**20


def fused_shards(
    hidden_in, attn_gain, qkv_weight, rel_bias, prefix_cache, prefix_owner, req_prefix,
    req_pages, page_table, proj_weight, mlp_gain, in_weight, out_weight,
):
    hidden = hidden_in[0]
    local, width = hidden.shape
    heads, dim = qkv_weight.shape[2:]
    inner = heads * dim
    tokens = 4 * local
    plen = prefix_cache.shape[1]
    dma = pltpu.SemaphoreType.DMA
    bf16, f32 = jnp.bfloat16, jnp.float32
    qkv, picked = pl.pallas_call(
        qkv_kernel,
        out_shape=(
            jax.ShapeDtypeStruct((tokens, 3 * inner), bf16),
            jax.ShapeDtypeStruct((2, plen, 2 * inner), bf16),
        ),
        in_specs=[VMEM] * 4 + [SMEM] * 2,
        out_specs=(VMEM, VMEM),
        scratch_shapes=[
            pltpu.VMEM((4, local, width), bf16),
            pltpu.VMEM((8, plen, 2 * inner), bf16),
            dma((3,)), dma((3,)), dma((3,)), dma((3,)), dma((3,)), dma((3,)), dma((4,)), dma((4,)), dma,
        ],
        compiler_params=pltpu.CompilerParams(
            collective_id=0, has_side_effects=True, vmem_limit_bytes=LIMIT
        ),
    )(
        hidden, attn_gain.reshape(1, width), qkv_weight.reshape(width, 3 * inner),
        prefix_cache.reshape(plen, 2 * inner), prefix_owner, req_prefix,
    )
    attended = pl.pallas_call(
        attend_kernel,
        out_shape=jax.ShapeDtypeStruct((tokens, inner), bf16),
        in_specs=[VMEM] * 2 + [SMEM] * 3,
        out_specs=VMEM,
        scratch_shapes=[
            pltpu.VMEM((tokens, 3 * inner), bf16),
            pltpu.VMEM((tokens, inner), bf16),
            pltpu.VMEM((heads, 5, TILE, TILE), f32),
            pltpu.VMEM((heads, 2 * tokens, TILE), f32),
        ],
        compiler_params=pltpu.CompilerParams(vmem_limit_bytes=LIMIT),
    )(qkv, picked, page_table, req_pages, rel_bias)
    hidden_out = pl.pallas_call(
        mlp_kernel,
        out_shape=jax.ShapeDtypeStruct((local, width), bf16),
        in_specs=[VMEM, VMEM, HBM, VMEM, HBM, HBM],
        out_specs=VMEM,
        scratch_shapes=[
            pltpu.VMEM(proj_weight.shape, bf16),
            pltpu.VMEM(in_weight.shape, bf16),
            pltpu.VMEM(out_weight.shape, bf16),
            pltpu.VMEM((4, local, inner), bf16),
            pltpu.VMEM((4, local, width), bf16),
            pltpu.VMEM((local, width), f32),
            pltpu.VMEM((local, width), f32),
            pltpu.VMEM((3, local, width), bf16),
            pltpu.VMEM((3, local, width), bf16),
            dma((3,)), dma((3,)), dma((3,)), dma((3,)), dma((3,)), dma((3,)), dma((3,)),
        ],
        compiler_params=pltpu.CompilerParams(
            collective_id=1, has_side_effects=True, vmem_limit_bytes=LIMIT
        ),
    )(hidden, attended, proj_weight, mlp_gain.reshape(1, width), in_weight, out_weight)
    suffix_cache = qkv[:, inner:].reshape(1, tokens, 2, heads, dim)
    return hidden_out[None], suffix_cache


def solution(mesh):
    return jax.shard_map(
        fused_shards if (mesh.shape["grp"], mesh.shape["blk"]) == (4, 8) else shards,
        mesh=mesh,
        in_specs=(
            P("blk", "grp", None),
            P(),
            P(None, None, "grp", None),
            P(None, "grp"),
            P("blk", None, None, "grp", None),
            P(),
            P(),
            P(),
            P(),
            P(),
            P(),
            P(None, "grp"),
            P("grp", None),
        ),
        out_specs=(P("blk", "grp", None), P("blk", None, None, "grp", None)),
        check_vma=False,
    )
```

```python
import jax
import jax.numpy as jnp
from jax import lax
from jax.experimental import pallas as pl
from jax.experimental.pallas import tpu as pltpu
from jax.sharding import PartitionSpec as P

PAGE = 32


EPSILON = 1e-06
THRESHOLDS = (12, 16, 23, 32, 46, 64, 91)


def rms_scale(values, gain):
    mean_sq = jnp.mean(values * values, axis=-1, keepdims=True)
    return values * lax.rsqrt(mean_sq + EPSILON) * gain


def bucket_of(relative):
    magnitude = jnp.abs(relative)
    steps_up = jnp.zeros(relative.shape, jnp.int32)
    for limit in THRESHOLDS:
        steps_up = steps_up + (magnitude >= limit).astype(jnp.int32)
    bucket = jnp.where(magnitude < 8, magnitude, jnp.minimum(8 + steps_up, 15))
    return bucket + 16 * (relative > 0).astype(jnp.int32)


def token_meta(pages_row, lengths_row, page_size, prefix_len):
    order = jnp.arange(lengths_row.shape[0], dtype=jnp.int32)
    inclusive = jnp.sum(
        jnp.where(order[None, :] <= order[:, None], lengths_row[None, :], 0), axis=1, dtype=jnp.int32
    )
    exclusive = inclusive - lengths_row
    request = jnp.sum(
        (pages_row[:, None] >= inclusive[None, :]).astype(jnp.int32), axis=1, dtype=jnp.int32
    )
    slot_ids = jnp.arange(lengths_row.shape[0], dtype=jnp.int32)
    start = jnp.sum(
        jnp.where(request[:, None] == slot_ids[None, :], exclusive[None, :], 0),
        axis=1,
        dtype=jnp.int32,
    )
    offsets = (pages_row - start) * page_size + prefix_len
    within = jnp.arange(page_size, dtype=jnp.int32)
    positions = (offsets[:, None] + within[None, :]).reshape(-1)
    requests = jnp.broadcast_to(request[:, None], (request.shape[0], page_size)).reshape(-1)
    return (requests, positions)


def attend_block(queries, key_rows, value_rows, query_req, query_pos, key_req, key_pos, rel_bias):
    scores = jnp.einsum("qhd,khd->hqk", queries, key_rows, preferred_element_type=jnp.float32)
    bucket = bucket_of(key_pos[None, :] - query_pos[:, None])
    bias_add = jnp.zeros(scores.shape, jnp.float32)
    for bucket_id in range(rel_bias.shape[0]):
        bias_add = jnp.where(
            (bucket == bucket_id)[None], rel_bias[bucket_id][:, None, None], bias_add
        )
    allowed = (key_req[None, :] == query_req[:, None])[None]
    scores = jnp.where(allowed, scores + bias_add, -1e30)
    row_max = jnp.max(scores, axis=-1, keepdims=True)
    weights = jnp.exp(scores - row_max)
    weights = (weights / jnp.sum(weights, axis=-1, keepdims=True)).astype(jnp.bfloat16)
    return jnp.einsum(
        "hqk,khd->qhd", weights, value_rows, preferred_element_type=jnp.float32
    ).astype(jnp.bfloat16)


def shards(
    hidden_in,
    attn_gain,
    qkv_weight,
    rel_bias,
    prefix_cache,
    prefix_owner,
    req_prefix,
    req_pages,
    page_table,
    proj_weight,
    mlp_gain,
    in_weight,
    out_weight,
):
    width = hidden_in.shape[2]
    heads_dev = qkv_weight.shape[2]
    head_dim = qkv_weight.shape[3]
    inner = heads_dev * head_dim
    residual = hidden_in[0].astype(jnp.float32)
    normed = rms_scale(residual, attn_gain).astype(jnp.bfloat16)
    qkv_flat = qkv_weight.reshape(width, 3 * inner)
    projected = jnp.dot(
        lax.all_gather(normed, "grp", axis=0, tiled=True),
        qkv_flat,
        preferred_element_type=jnp.float32,
    ).astype(jnp.bfloat16)
    column_tok = projected.shape[0]
    projected = projected.reshape(column_tok, 3, heads_dev, head_dim)
    suffix_cache = projected[:, 1:3][None]
    column = lax.axis_index("blk")
    requests_col = req_prefix.shape[1]
    prefix_ids = jnp.arange(prefix_owner.shape[0], dtype=jnp.int32)
    owner_cols = jnp.sum(
        jnp.where(
            req_prefix[:, :, None] == prefix_ids[None, None, :], prefix_owner[None, None, :], 0
        ),
        axis=2,
        dtype=jnp.int32,
    )
    my_cols = lax.dynamic_index_in_dim(owner_cols, column, 0, keepdims=False)
    prefix_len = prefix_cache.shape[1]
    slot_width = 2 * inner
    local_slot = prefix_cache.reshape(prefix_len, slot_width)
    gathered = lax.all_gather(local_slot[None], "blk", axis=0, tiled=True)
    prefix_rows = jnp.stack(
        [
            lax.dynamic_index_in_dim(gathered, my_cols[k], 0, keepdims=False)
            for k in range(requests_col)
        ]
    )
    prefix_rows = prefix_rows.reshape(requests_col * prefix_len, 2, heads_dev, head_dim)
    key_rows = jnp.concatenate([prefix_rows[:, 0], projected[:, 1]], axis=0)
    value_rows = jnp.concatenate([prefix_rows[:, 1], projected[:, 2]], axis=0)
    pages_row = lax.dynamic_index_in_dim(page_table, column, 0, keepdims=False)
    lengths_row = lax.dynamic_index_in_dim(req_pages, column, 0, keepdims=False)
    query_req, query_pos = token_meta(pages_row, lengths_row, PAGE, prefix_len)
    slot_ids = jnp.arange(requests_col, dtype=jnp.int32)
    key_req = jnp.concatenate([jnp.repeat(slot_ids, prefix_len), query_req])
    key_pos = jnp.concatenate(
        [jnp.tile(jnp.arange(prefix_len, dtype=jnp.int32), requests_col), query_pos]
    )
    block_rows = min(512, column_tok)
    block_count = column_tok // block_rows

    def one_block(operands):
        block_q, block_req, block_pos = operands
        return attend_block(
            block_q, key_rows, value_rows, block_req, block_pos, key_req, key_pos, rel_bias
        )

    attended = lax.map(
        one_block,
        (
            projected[:, 0].reshape(block_count, block_rows, heads_dev, head_dim),
            query_req.reshape(block_count, block_rows),
            query_pos.reshape(block_count, block_rows),
        ),
    )
    attended = attended.reshape(1, column_tok, inner)
    token_heads = lax.all_to_all(attended, "grp", split_axis=1, concat_axis=2, tiled=True)[0]
    mixed = residual + jnp.dot(token_heads, proj_weight, preferred_element_type=jnp.float32)
    normed_mlp = rms_scale(mixed, mlp_gain).astype(jnp.bfloat16)
    activated = jax.nn.relu(
        jnp.dot(
            lax.all_gather(normed_mlp, "grp", axis=0, tiled=True),
            in_weight,
            preferred_element_type=jnp.float32,
        )
    ).astype(jnp.bfloat16)
    summed = lax.psum_scatter(
        jnp.dot(activated, out_weight, preferred_element_type=jnp.float32).astype(jnp.bfloat16),
        "grp",
        scatter_dimension=0,
        tiled=True,
    ).astype(jnp.float32)
    hidden_out = (mixed + summed).astype(jnp.bfloat16)[None]
    return (hidden_out, suffix_cache)


MESH = pl.DeviceIdType.MESH
TILE = 128


def remote(src, dst, send, recv, where):
    return pltpu.make_async_remote_copy(
        src_ref=src, dst_ref=dst, send_sem=send, recv_sem=recv, device_id=where, device_id_type=MESH
    )


def grp_places():
    me = lax.axis_index("grp")
    y, core = me // 2, me % 2
    return me, y * 2 + 1 - core, (1 - y) * 2 + core, (1 - y) * 2 + 1 - core


def rms_rows(values, gain):
    mean_sq = jnp.mean(values * values, axis=-1, keepdims=True)
    return (values * lax.rsqrt(mean_sq + EPSILON) * gain).astype(jnp.bfloat16)


def qkv_kernel(
    hidden, gain, weight, prefix, owner, req_prefix,
    qkv, picked,
    states, slots, g_send, g_recv, r_send, r_recv, l_send, l_recv, x_send, x_recv, own_sem,
):
    me, mate, across, diag = grp_places()
    blk = lax.axis_index("blk")
    z, x = blk // 2, blk % 2
    other = z * 2 + 1 - x
    mine = pltpu.make_async_copy(prefix, slots.at[blk], own_sem)
    mine.start()
    barrier = pltpu.get_barrier_semaphore()
    for place in ({"grp": mate}, {"grp": across}, {"blk": other},
                  {"blk": (z + 1) % 4 * 2 + x}, {"blk": (z + 3) % 4 * 2 + x}):
        pl.semaphore_signal(barrier, inc=1, device_id=place, device_id_type=MESH)
    pl.semaphore_wait(barrier, 5)
    mine.wait()

    def up(slot, s):
        ref = slots.at[slot * 2 + x]
        return remote(ref, ref, r_send.at[s], r_recv.at[s], {"blk": (z + 1) % 4 * 2 + x})

    def down(slot, s):
        ref = slots.at[slot * 2 + x]
        return remote(ref, ref, l_send.at[s], l_recv.at[s], {"blk": (z + 3) % 4 * 2 + x})

    def over(slot, side):
        ref = slots.at[slot * 2 + side]
        return remote(ref, ref, x_send.at[slot], x_recv.at[slot], {"blk": other})

    def hop(s):
        @pl.when((z < 3) & (z >= s))
        def _():
            up(z - s, s).start()

        @pl.when((z > 0) & (z + s <= 3))
        def _():
            down(z + s, s).start()

    def land(s):
        @pl.when(z >= s + 1)
        def _():
            up(z - 1 - s, s).wait_recv()

        @pl.when(z + s + 1 <= 3)
        def _():
            down(z + 1 + s, s).wait_recv()

        if s < 2:
            hop(s + 1)

        @pl.when(z >= s + 1)
        def _():
            over(z - 1 - s, x).start()

        @pl.when(z + s + 1 <= 3)
        def _():
            over(z + 1 + s, x).start()

    hop(0)
    over(z, x).start()
    states[me] = rms_rows(hidden[...].astype(jnp.float32), gain[...])
    to_mate = remote(states.at[me], states.at[me], g_send.at[0], g_recv.at[0], {"grp": mate})
    to_across = remote(states.at[me], states.at[me], g_send.at[1], g_recv.at[1], {"grp": across})
    to_across.start()
    to_mate.start()

    def project(place):
        rows = pl.ds(pl.multiple_of(place * TILE, TILE), TILE)
        qkv[rows, :] = jnp.dot(
            states[place], weight[...], preferred_element_type=jnp.float32
        ).astype(jnp.bfloat16)

    project(me)
    remote(states.at[mate], states.at[mate], g_send.at[0], g_recv.at[0], {"grp": mate}).wait_recv()
    project(mate)
    remote(states.at[across], states.at[across], g_send.at[1], g_recv.at[1], {"grp": across}).wait_recv()
    onward = remote(states.at[across], states.at[across], g_send.at[2], g_recv.at[2], {"grp": mate})
    onward.start()
    land(0)
    project(across)
    remote(states.at[diag], states.at[diag], g_send.at[2], g_recv.at[2], {"grp": mate}).wait_recv()
    project(diag)
    land(1)
    land(2)
    for slot in range(4):
        over(slot, 1 - x).wait_recv()
    for k in range(2):
        picked[k] = slots[owner[req_prefix[blk, k]]]
    to_mate.wait_send()
    to_across.wait_send()
    onward.wait_send()
    for s in range(3):
        @pl.when((z < 3) & (z >= s))
        def _():
            up(z - s, s).wait_send()

        @pl.when((z > 0) & (z + s <= 3))
        def _():
            down(z + s, s).wait_send()
    for slot in range(4):
        over(slot, x).wait_send()


def attend_kernel(qkv, picked, pages, lengths, rel_bias, out, ordered, result, tiles, shifted):
    blk = lax.axis_index("blk")
    tokens, inner = out.shape
    page_count = tokens // PAGE
    heads = rel_bias.shape[1]
    dim = inner // heads
    split = lengths[blk, 0] * PAGE
    row = lax.broadcasted_iota(jnp.int32, (TILE, TILE), 0)
    col = lax.broadcasted_iota(jnp.int32, (TILE, TILE), 1)

    @pl.loop(1, 4)
    def _(d):
        bucket = bucket_of((d - 2) * TILE + col - row)
        sums = [jnp.zeros((TILE, TILE), jnp.float32)] * heads
        for b in range(rel_bias.shape[0]):
            here = bucket == b
            sums = [jnp.where(here, rel_bias[b, h], sums[h]) for h in range(heads)]
        for h in range(heads):
            tiles[h, d] = sums[h]

    for h in range(heads):
        tiles[h, 0] = jnp.full((TILE, TILE), rel_bias[15, h], jnp.float32)
        tiles[h, 4] = jnp.full((TILE, TILE), rel_bias[31, h], jnp.float32)
        shifted[h] = jnp.full((2 * tokens, TILE), rel_bias[15, h], jnp.float32)
        shifted[h, tokens:tokens + TILE] = tiles[h, 1]

    @pl.loop(0, page_count)
    def _(logical):
        physical = jnp.int32(0)
        for j in range(page_count):
            physical = physical + jnp.where(pages[blk, j] == logical, j, 0)
        ordered[pl.ds(pl.multiple_of(logical * PAGE, PAGE), PAGE), :] = qkv[
            pl.ds(pl.multiple_of(physical * PAGE, PAGE), PAGE), :
        ]

    blocks = tokens // TILE
    key_late = lax.broadcasted_iota(jnp.int32, (TILE, tokens), 1) >= split

    @pl.loop(0, blocks)
    def _(i):
        rows = pl.ds(pl.multiple_of(i * TILE, TILE), TILE)
        number = i * TILE + lax.broadcasted_iota(jnp.int32, (TILE, tokens), 0)
        allowed = (number >= split) == key_late
        late = i * TILE + lax.broadcasted_iota(jnp.int32, (TILE, 2 * TILE), 0) >= split
        shift = pl.multiple_of(tokens + i * TILE - split, PAGE)
        contract = (((1,), (1,)), ((), ()))
        for h in range(heads):
            at = slice(h * dim, (h + 1) * dim)
            key_at = slice(inner + h * dim, inner + (h + 1) * dim)
            value_at = slice(2 * inner + h * dim, 2 * inner + (h + 1) * dim)
            q = ordered[rows, at]

            def against(keys):
                return lax.dot_general(q, keys, contract, preferred_element_type=jnp.float32)

            own = against(ordered[:, key_at])
            bias = jnp.concatenate(
                [tiles[h, jnp.clip(j - i, -2, 2) + 2] for j in range(blocks)], axis=1
            )
            own = jnp.where(allowed, own + bias, -1e30)
            far = jnp.full((TILE, TILE), rel_bias[15, h], jnp.float32)
            early = jnp.concatenate([far, tiles[h, jnp.maximum(1 - i, 0)]], axis=1)
            later = jnp.concatenate([far, shifted[h, pl.ds(shift, TILE), :]], axis=1)
            before = jnp.where(
                late, against(picked[1, :, at]) + later, against(picked[0, :, at]) + early
            )
            top = jnp.maximum(
                jnp.max(own, axis=1, keepdims=True), jnp.max(before, axis=1, keepdims=True)
            )
            own = jnp.exp(own - top)
            before = jnp.exp(before - top)
            total = jnp.sum(own, axis=1, keepdims=True) + jnp.sum(before, axis=1, keepdims=True)
            summed = jnp.dot(
                own.astype(jnp.bfloat16), ordered[:, value_at], preferred_element_type=jnp.float32
            )
            for k in range(2):
                part = jnp.where(late == (k == 1), before, 0.0).astype(jnp.bfloat16)
                summed = summed + jnp.dot(
                    part, picked[k, :, key_at], preferred_element_type=jnp.float32
                )
            result[rows, at] = (summed / total).astype(jnp.bfloat16)

    @pl.loop(0, page_count)
    def _(j):
        out[pl.ds(pl.multiple_of(j * PAGE, PAGE), PAGE), :] = result[
            pl.ds(pl.multiple_of(pages[blk, j] * PAGE, PAGE), PAGE), :
        ]


def mlp_kernel(
    hidden, attended, proj_hbm, gain, in_hbm, out_hbm,
    final,
    proj, in_w, out_w, heads_in, states, mixed, total, leaving, arriving,
    w_sem, a_send, a_recv, g_send, g_recv, s_send, s_recv,
):
    me, mate, across, diag = grp_places()
    loads = [
        pltpu.make_async_copy(a, b, w_sem.at[k])
        for k, (a, b) in enumerate(((proj_hbm, proj), (in_hbm, in_w), (out_hbm, out_w)))
    ]
    for load in loads:
        load.start()
    barrier = pltpu.get_barrier_semaphore()
    for place in (mate, across, diag):
        pl.semaphore_signal(barrier, inc=1, device_id={"grp": place}, device_id_type=MESH)
    pl.semaphore_wait(barrier, 3)

    def rows_of(place):
        return pl.ds(pl.multiple_of(place * TILE, TILE), TILE)

    def share_out(k, place):
        return remote(
            attended.at[rows_of(place), :], heads_in.at[me], a_send.at[k], a_recv.at[k], {"grp": place}
        )

    def share_in(k, place):
        return remote(
            attended.at[rows_of(place), :], heads_in.at[place], a_send.at[k], a_recv.at[k], {"grp": place}
        )

    peers = ((1, across), (2, diag), (0, mate))
    for k, place in peers:
        share_out(k, place).start()
    depth = attended.shape[1]

    def mix(block, place):
        return jnp.dot(
            block,
            proj[pl.ds(pl.multiple_of(place * depth, depth), depth), :],
            preferred_element_type=jnp.float32,
        )

    loads[0].wait()
    mixed[...] = hidden[...].astype(jnp.float32) + mix(attended[rows_of(me), :], me)
    for k, place in ((0, mate), (1, across), (2, diag)):
        share_in(k, place).wait_recv()
        mixed[...] += mix(heads_in[place], place)
    states[me] = rms_rows(mixed[...], gain[...])
    to_mate = remote(states.at[me], states.at[me], g_send.at[0], g_recv.at[0], {"grp": mate})
    to_across = remote(states.at[me], states.at[me], g_send.at[1], g_recv.at[1], {"grp": across})
    to_across.start()
    to_mate.start()
    loads[1].wait()
    loads[2].wait()

    def share(place):
        hidden_units = jnp.dot(states[place], in_w[...], preferred_element_type=jnp.float32)
        activated = jnp.maximum(hidden_units, 0.0).astype(jnp.bfloat16)
        return jnp.dot(activated, out_w[...], preferred_element_type=jnp.float32)

    def give(k, place):
        return remote(leaving.at[k], arriving.at[k], s_send.at[k], s_recv.at[k], {"grp": place})

    total[...] = share(me)
    remote(states.at[mate], states.at[mate], g_send.at[0], g_recv.at[0], {"grp": mate}).wait_recv()
    leaving[0] = share(mate).astype(jnp.bfloat16)
    give(0, mate).start()
    total[...] += mixed[...]
    remote(states.at[across], states.at[across], g_send.at[1], g_recv.at[1], {"grp": across}).wait_recv()
    onward = remote(states.at[across], states.at[across], g_send.at[2], g_recv.at[2], {"grp": mate})
    onward.start()
    mixed[...] = share(across)
    remote(states.at[diag], states.at[diag], g_send.at[2], g_recv.at[2], {"grp": mate}).wait_recv()
    leaving[1] = share(diag).astype(jnp.bfloat16)
    give(1, mate).start()
    give(1, mate).wait_recv()
    leaving[2] = (mixed[...] + arriving[1].astype(jnp.float32)).astype(jnp.bfloat16)
    give(2, across).start()
    give(0, mate).wait_recv()
    total[...] += arriving[0].astype(jnp.float32)
    give(2, across).wait_recv()
    final[...] = (total[...] + arriving[2].astype(jnp.float32)).astype(jnp.bfloat16)
    for k, place in peers:
        share_out(k, place).wait_send()
    to_mate.wait_send()
    to_across.wait_send()
    onward.wait_send()
    give(0, mate).wait_send()
    give(1, mate).wait_send()
    give(2, across).wait_send()


VMEM = pl.BlockSpec(memory_space=pltpu.VMEM)
SMEM = pl.BlockSpec(memory_space=pltpu.SMEM)
HBM = pl.BlockSpec(memory_space=pl.ANY)
LIMIT = 48 * 2**20


def fused_shards(
    hidden_in, attn_gain, qkv_weight, rel_bias, prefix_cache, prefix_owner, req_prefix,
    req_pages, page_table, proj_weight, mlp_gain, in_weight, out_weight,
):
    hidden = hidden_in[0]
    local, width = hidden.shape
    heads, dim = qkv_weight.shape[2:]
    inner = heads * dim
    tokens = 4 * local
    plen = prefix_cache.shape[1]
    dma = pltpu.SemaphoreType.DMA
    bf16, f32 = jnp.bfloat16, jnp.float32
    qkv, picked = pl.pallas_call(
        qkv_kernel,
        out_shape=(
            jax.ShapeDtypeStruct((tokens, 3 * inner), bf16),
            jax.ShapeDtypeStruct((2, plen, 2 * inner), bf16),
        ),
        in_specs=[VMEM] * 4 + [SMEM] * 2,
        out_specs=(VMEM, VMEM),
        scratch_shapes=[
            pltpu.VMEM((4, local, width), bf16),
            pltpu.VMEM((8, plen, 2 * inner), bf16),
            dma((3,)), dma((3,)), dma((3,)), dma((3,)), dma((3,)), dma((3,)), dma((4,)), dma((4,)), dma,
        ],
        compiler_params=pltpu.CompilerParams(
            collective_id=0, has_side_effects=True, vmem_limit_bytes=LIMIT
        ),
    )(
        hidden, attn_gain.reshape(1, width), qkv_weight.reshape(width, 3 * inner),
        prefix_cache.reshape(plen, 2 * inner), prefix_owner, req_prefix,
    )
    attended = pl.pallas_call(
        attend_kernel,
        out_shape=jax.ShapeDtypeStruct((tokens, inner), bf16),
        in_specs=[VMEM] * 2 + [SMEM] * 3,
        out_specs=VMEM,
        scratch_shapes=[
            pltpu.VMEM((tokens, 3 * inner), bf16),
            pltpu.VMEM((tokens, inner), bf16),
            pltpu.VMEM((heads, 5, TILE, TILE), f32),
            pltpu.VMEM((heads, 2 * tokens, TILE), f32),
        ],
        compiler_params=pltpu.CompilerParams(vmem_limit_bytes=LIMIT),
    )(qkv, picked, page_table, req_pages, rel_bias)
    hidden_out = pl.pallas_call(
        mlp_kernel,
        out_shape=jax.ShapeDtypeStruct((local, width), bf16),
        in_specs=[VMEM, VMEM, HBM, VMEM, HBM, HBM],
        out_specs=VMEM,
        scratch_shapes=[
            pltpu.VMEM(proj_weight.shape, bf16),
            pltpu.VMEM(in_weight.shape, bf16),
            pltpu.VMEM(out_weight.shape, bf16),
            pltpu.VMEM((4, local, inner), bf16),
            pltpu.VMEM((4, local, width), bf16),
            pltpu.VMEM((local, width), f32),
            pltpu.VMEM((local, width), f32),
            pltpu.VMEM((3, local, width), bf16),
            pltpu.VMEM((3, local, width), bf16),
            dma((3,)), dma((3,)), dma((3,)), dma((3,)), dma((3,)), dma((3,)), dma((3,)),
        ],
        compiler_params=pltpu.CompilerParams(
            collective_id=1, has_side_effects=True, vmem_limit_bytes=60 * 2**20
        ),
    )(hidden, attended, proj_weight, mlp_gain.reshape(1, width), in_weight, out_weight)
    suffix_cache = qkv[:, inner:].reshape(1, tokens, 2, heads, dim)
    return hidden_out[None], suffix_cache


def solution(mesh):
    return jax.shard_map(
        fused_shards if (mesh.shape["grp"], mesh.shape["blk"]) == (4, 8) else shards,
        mesh=mesh,
        in_specs=(
            P("blk", "grp", None),
            P(),
            P(None, None, "grp", None),
            P(None, "grp"),
            P("blk", None, None, "grp", None),
            P(),
            P(),
            P(),
            P(),
            P(),
            P(),
            P(None, "grp"),
            P("grp", None),
        ),
        out_specs=(P("blk", "grp", None), P("blk", None, None, "grp", None)),
        check_vma=False,
    )
```
